32 devices in a mesh: dp: 8 (over z, x), mp: 4 (over y, core).
Axes of the slice: x: 2, y: 2, z: 4, core: 2. Of those that a mesh axis runs over, the one named last changes fastest.
Arguments:
- query: bfloat16 [2048, 4096], P('dp', 'mp'), may hold values from -400 to 400
- keys_values: bfloat16 [2, 2048, 512], P(None, 'dp'), may hold values from -6 to 6
- ancestors: int32 [16, 12], P('dp'), may hold values from -1 to 15, as said below
- tile_of_slot: int32 [16], replicated, may hold values from 0 to 15, as said below
- residual: bfloat16 [2048, 8192], P('dp', 'mp'), may hold values from -6 to 6
- norm_gain: float32 [8192], P('mp'), may hold values from 0.25 to 1.75
- out_weight: bfloat16 [4096, 8192], P('mp'), may hold values from -0.09375 to 0.09375
Outputs:
- hidden_out: bfloat16 [2048, 8192], P('dp', 'mp')
- normed: bfloat16 [2048, 8192], P('dp', 'mp')
The draws below stay inside these ranges and needn't reach their ends.
Inputs may be any that keep to these rules, and one draw needn't show every extreme that they name: Ids of tiles, or -1. Over all query tiles of one device's 2 positions, the ancestors that lie at the positions of any one device number at most 1 distinct tiles; some device reaches 1 in every draw. `tile_of_slot`: a permutation of the tile ids.
All inputs are finite; a program needn't handle non-finite values.
Results may differ from the reference program's by a relative error of at most 0.008.
Values may be sent and summed in bfloat16 or wider, within the bound.
A program may use at most 64 MiB of HBM per device.

```python
import jax
import jax.numpy as jnp
from jax import lax

D = 8192
HEADS = 32
KV_HEADS = 4
HEAD = 128
TILE = 128
ANC = 12
TILES_DEV = 2
TILES = 16
TOKENS = 2048
N_MP = 4


def attention_inputs(key):
    queries = jax.random.normal(jax.random.fold_in(key, 201), (TOKENS, HEADS, HEAD), jnp.float32)
    pairs = jax.random.normal(jax.random.fold_in(key, 202), (2, TOKENS, KV_HEADS, HEAD), jnp.float32)
    queries = jnp.clip(queries, -6.0, 6.0)
    pairs = jnp.clip(pairs, -6.0, 6.0)
    return (queries.reshape(TOKENS, HEADS * HEAD).astype(jnp.bfloat16), pairs.reshape(2, TOKENS, KV_HEADS * HEAD).astype(jnp.bfloat16))


def tile_plan(key):
    devices = TILES // TILES_DEV
    permuted = jax.random.permutation(jax.random.fold_in(key, 101), TILES).astype(jnp.int32)
    window_start = jax.random.randint(jax.random.fold_in(key, 102), (devices, devices), 0, TILES_DEV)
    order_keys = jax.random.split(jax.random.fold_in(key, 103), devices)
    orders = jax.vmap(lambda one_key: jax.random.permutation(one_key, devices))(order_keys).astype(jnp.int32)
    home_dev = jnp.arange(TILES) // TILES_DEV
    local_index = jnp.arange(TILES) % TILES_DEV
    flat_entry = local_index[:, None] * ANC + jnp.arange(ANC)[None, :]
    source = orders[home_dev[:, None], flat_entry % devices]
    offset = window_start[home_dev[:, None], source]
    slot_ids = source * TILES_DEV + offset
    live_count = jax.random.randint(jax.random.fold_in(key, 105), (TILES,), max(2, ANC - 4), ANC + 1)
    heavy = home_dev % 4 == 0
    live_count = jnp.where(heavy, ANC, live_count)
    is_live = jnp.arange(ANC)[None, :] < live_count[:, None]
    tile_ids = jnp.where(is_live, permuted[slot_ids], -1)
    return (permuted, tile_ids.astype(jnp.int32))


def draw_query(key, part):
    return attention_inputs(key)[0]


def draw_keys_values(key, part):
    return attention_inputs(key)[1]


def draw_ancestors(key, part):
    return tile_plan(key)[1]


def draw_tile_of_slot(key, part):
    return tile_plan(key)[0]


def steps_of(key, dims, cuts, low, high):
    gain, own = 1.0, jax.random.fold_in(key, 6)
    for position, parts in cuts:
        heights = jnp.exp(jax.random.uniform(jax.random.fold_in(own, position), (parts,), jnp.float32, low / len(cuts), high / len(cuts)))
        gain = gain * jnp.repeat(heights, dims[position] // parts).reshape([-1 if axis == position else 1 for axis in range(len(dims))])
    return gain


def noise(stream_key, shape, width, limit, shards=(), kind=jnp.bfloat16):
    loudness = steps_of(stream_key, shape, shards, -0.22, 0.18) if shards else 1.0
    entries = jax.random.normal(stream_key, shape, jnp.float32) * width * loudness
    return jnp.minimum(jnp.maximum(entries, -limit), limit).astype(kind)


def setup_inputs(seed: int = 0) -> dict:
    arg_keys = jax.random.split(jax.random.key(seed), 8)
    return {
        "query": draw_query(jax.random.fold_in(arg_keys[7], 71), 0),
        "keys_values": draw_keys_values(jax.random.fold_in(arg_keys[7], 71), 0),
        "ancestors": draw_ancestors(jax.random.fold_in(arg_keys[7], 71), 0),
        "tile_of_slot": draw_tile_of_slot(jax.random.fold_in(arg_keys[7], 71), 0),
        "residual": noise(arg_keys[4], (TOKENS, D), 1.0, 6.0, ((0, 8), (1, 4))),
        "norm_gain": jnp.clip(1.0 + 0.15 * jax.random.normal(arg_keys[5], (D,), jnp.float32), 0.25, 1.75),
        "out_weight": noise(arg_keys[6], (HEADS * HEAD, D), (HEADS * HEAD) ** -0.5, 0.09375, ((0, 4),)),
    }


def slot_table(tile_of_slot, tile_count):
    numbers = jnp.arange(tile_count, dtype=jnp.int32)
    matches = tile_of_slot[None, :] == numbers[:, None]
    return lax.optimization_barrier(jnp.sum(jnp.where(matches, numbers[None, :], 0), axis=1)).astype(jnp.int32)

def live_slots(ancestors, slot_of, own_slots, tile_count):
    numbers = jnp.arange(tile_count, dtype=jnp.int32)
    matches = ancestors[:, :, None] == numbers[None, None, :]
    located = lax.optimization_barrier(jnp.sum(jnp.where(matches, slot_of[None, None, :], 0), axis=2)).astype(jnp.int32)
    located = jnp.where(ancestors >= 0, located, -1).astype(jnp.int32)
    width_anc = ancestors.shape[1]
    before = jnp.arange(width_anc)[:, None] > jnp.arange(width_anc)[None, :]
    repeated = jnp.any((located[:, :, None] == located[:, None, :]) & before[None], axis=2)
    keeping = (located >= 0) & (located != own_slots[:, None]) & jnp.logical_not(repeated)
    return jnp.where(keeping, located, -1).astype(jnp.int32)

def tile_attention(query_tile, key_own, value_own, key_far, value_far, far_live):
    kv_heads = key_own.shape[1]
    group_size = query_tile.shape[1] // (kv_heads * HEAD)
    score_scale = HEAD ** (-0.5)
    query_grid = query_tile.astype(jnp.float32).reshape(TILE, kv_heads, group_size, HEAD)
    near = jnp.einsum('qhgd,khd->hgqk', query_grid, key_own.astype(jnp.float32)) * score_scale
    causal = jnp.arange(TILE)[:, None] >= jnp.arange(TILE)[None, :]
    near = jnp.where(causal, near, -jnp.inf)
    far = jnp.einsum('qhgd,akhd->hgqak', query_grid, key_far.astype(jnp.float32)) * score_scale
    far = jnp.where(far_live[None, None, None, :, None], far, -jnp.inf)
    peak = jnp.maximum(lax.optimization_barrier(jnp.max(near, axis=3)), lax.optimization_barrier(jnp.max(far, axis=(3, 4))))
    near_weight = jnp.exp(near - peak[..., None])
    far_weight = jnp.exp(far - peak[..., None, None])
    totals = lax.optimization_barrier(jnp.sum(near_weight, axis=3)) + lax.optimization_barrier(jnp.sum(far_weight, axis=(3, 4)))
    near_round = lax.optimization_barrier(near_weight.astype(jnp.bfloat16)).astype(jnp.float32)
    far_round = lax.optimization_barrier(far_weight.astype(jnp.bfloat16)).astype(jnp.float32)
    mixed = jnp.einsum('hgqk,khd->hgqd', near_round, value_own.astype(jnp.float32))
    mixed = mixed + jnp.einsum('hgqak,akhd->hgqd', far_round, value_far.astype(jnp.float32))
    mixed = mixed / totals[..., None]
    return jnp.transpose(mixed, (2, 0, 1, 3)).reshape(TILE, kv_heads * group_size * HEAD).astype(jnp.bfloat16)

def reference(query, keys_values, ancestors, tile_of_slot, residual, norm_gain, out_weight):
    slot_of = slot_table(tile_of_slot, TILES)
    far_slots = live_slots(ancestors, slot_of, jnp.arange(TILES, dtype=jnp.int32), TILES)
    query_tiles = query.reshape(TILES, TILE, HEADS * HEAD)
    key_tiles = keys_values[0].reshape(TILES, TILE, KV_HEADS, HEAD)
    value_tiles = keys_values[1].reshape(TILES, TILE, KV_HEADS, HEAD)

    def one_tile(index):
        picked = jnp.clip(far_slots[index], 0, TILES - 1)
        return tile_attention(query_tiles[index], key_tiles[index], value_tiles[index], key_tiles[picked], value_tiles[picked], far_slots[index] >= 0)
    attended = lax.map(one_tile, jnp.arange(TILES, dtype=jnp.int32)).reshape(TOKENS, HEADS * HEAD)
    block_width = HEADS * HEAD // N_MP
    projected = jnp.zeros((TOKENS, D), jnp.float32)
    for block in range(N_MP):
        partial_term = jnp.dot(attended[:, block * block_width:(block + 1) * block_width], out_weight[block * block_width:(block + 1) * block_width], preferred_element_type=jnp.float32)
        partial_term = lax.optimization_barrier(partial_term.astype(jnp.bfloat16)).astype(jnp.float32)
        projected = projected + partial_term
    hidden_out = (residual.astype(jnp.float32) + projected).astype(jnp.bfloat16)
    hidden_f32 = hidden_out.astype(jnp.float32)
    mean_sq = lax.optimization_barrier(jnp.mean(hidden_f32 * hidden_f32, axis=1))
    normed = hidden_f32 * lax.rsqrt(mean_sq + 1e-05)[:, None] * norm_gain[None, :]
    return (hidden_out, normed.astype(jnp.bfloat16))
```

```python
import functools
import math

import jax
import jax.numpy as jnp
from jax import lax
from jax.experimental import pallas as pl
from jax.experimental.pallas import tpu as pltpu
from jax.sharding import PartitionSpec as P

HEAD = 128
TILE = 128
WIDTH = 512
F32 = jnp.float32
BF16 = jnp.bfloat16
MESH = pl.DeviceIdType.MESH


def kernel(
    sizes,
    anc_ref, slots_ref, query_ref, pairs_ref, residual_ref, gain_ref, weight_ref,
    hidden_ref, normed_ref,
    kv, keys, values, bias, q, res, gain, w, att, near_send, near_recv,
    far_send, far_recv, own, hid, nrm, sq_send, sq_recv,
    load_sem, w_sem, out_sem, kv_recv_sem, kv_z_sem, kv_x_sem,
    near_send_sem, near_recv_sem, far_send_sem, far_recv_sem, sq_send_sem, sq_recv_sem,
):
    dp_count, mp_count, nx, tiles, heads, kv_heads, width = sizes
    nz = dp_count // nx
    ny = mp_count // 2
    features = mp_count * width
    chunks = width // WIDTH
    me_dp, me_mp = lax.axis_index("dp"), lax.axis_index("mp")
    z, x = me_dp // nx, me_dp % nx
    y, core = me_mp // 2, me_mp % 2
    sibling = y * 2 + (1 - core)

    def dev(dp, mp):
        return {"dp": dp, "mp": mp}

    kv_head = me_mp * kv_heads // mp_count
    own_kv = pltpu.make_async_copy(
        pairs_ref.at[:, :, pl.ds(pl.multiple_of(kv_head * HEAD, HEAD), HEAD)],
        kv.at[me_dp], load_sem.at[0])
    own_kv.start()
    load_q = pltpu.make_async_copy(query_ref, q, load_sem.at[1])
    load_q.start()
    blocks = []
    for dy in list(range(1, ny)) + [0]:
        for other in (1, 0):
            block = ((y + dy) % ny) * 2 + (core if other == 0 else 1 - core)
            blocks.append(block)
    w_loads = []
    for i, block in enumerate(blocks):
        copy = pltpu.make_async_copy(
            weight_ref.at[:, pl.ds(pl.multiple_of(block * width, width), width)],
            w.at[i], w_sem.at[i])
        copy.start()
        w_loads.append(copy)
    load_res = pltpu.make_async_copy(residual_ref, res, load_sem.at[2])
    load_res.start()
    load_gain = pltpu.make_async_copy(gain_ref, gain, load_sem.at[3])
    load_gain.start()

    barrier = pltpu.get_barrier_semaphore()
    for dm in range(1, mp_count):
        pl.semaphore_signal(barrier, inc=1, device_id=dev(me_dp, (me_mp + dm) % mp_count), device_id_type=MESH)
    for dx in range(1, nx):
        pl.semaphore_signal(barrier, inc=1, device_id=dev(z * nx + (x + dx) % nx, me_mp), device_id_type=MESH)

    @pl.when(z > 0)
    def _():
        pl.semaphore_signal(barrier, inc=1, device_id=dev(me_dp - nx, me_mp), device_id_type=MESH)

    @pl.when(z < nz - 1)
    def _():
        pl.semaphore_signal(barrier, inc=1, device_id=dev(me_dp + nx, me_mp), device_id_type=MESH)

    ends = jnp.where(z > 0, 1, 0) + jnp.where(z < nz - 1, 1, 0)
    pl.semaphore_wait(barrier, mp_count - 1 + nx - 1 + ends)
    own_kv.wait()

    def kv_copy(src, target, send_sem):
        return pltpu.make_async_remote_copy(
            src_ref=kv.at[src], dst_ref=kv.at[src], send_sem=send_sem,
            recv_sem=kv_recv_sem.at[src], device_id=dev(target, me_mp), device_id_type=MESH)

    def z_send(line, up):
        return kv_copy(line * nx + x, me_dp + (nx if up else -nx), kv_z_sem.at[1 if up else 0, line])

    def x_send(line, dx):
        return kv_copy(line * nx + x, z * nx + (x + dx) % nx, kv_x_sem.at[dx - 1, line])

    @pl.when(z < nz - 1)
    def _():
        z_send(z, True).start()

    @pl.when(z > 0)
    def _():
        z_send(z, False).start()

    for dx in range(1, nx):
        x_send(z, dx).start()

    for t in range(tiles):
        bias[t, :, 0:TILE] = jnp.zeros((8, TILE), F32)

    def lookup(src, picks):
        seen = []
        for t in range(tiles):
            row = []
            for u in range(tiles):
                slot = src * tiles + u
                tile_id = slots_ref[slot]
                found = jnp.int32(0)
                for j in range(anc_ref.shape[1]):
                    found = found | jnp.where(anc_ref[t, j] == tile_id, 1, 0)
                found = found * jnp.where(slot == me_dp * tiles + t, 0, 1)
                row.append(found)
            seen.append(row)
        for t in range(tiles):
            hit = functools.reduce(lambda a, b: a | b, seen[t])
            column = jnp.where(jnp.full((8, TILE), hit) > 0, 0.0, -jnp.inf).astype(F32)
            bias[t, :, pl.ds(pl.multiple_of((src + 1) * TILE, TILE), TILE)] = column
        return tuple(
            tuple(jnp.where(i == src, functools.reduce(lambda a, b: a | b, [seen[t][u] for t in range(tiles)]), old)
                  for i, old in enumerate(picks[u]))
            for u in range(tiles))

    picks = lax.fori_loop(
        0, dp_count, lookup,
        tuple(tuple(jnp.int32(0) for _ in range(dp_count)) for _ in range(tiles)))

    for d in range(1, nz):
        @pl.when(z >= d)
        def _():
            line = z - d
            kv_copy(line * nx + x, me_dp, kv_z_sem.at[0, 0]).wait_recv()

            @pl.when(z < nz - 1)
            def _():
                z_send(line, True).start()

            for dx in range(1, nx):
                x_send(line, dx).start()

        @pl.when(z + d < nz)
        def _():
            line = z + d
            kv_copy(line * nx + x, me_dp, kv_z_sem.at[0, 0]).wait_recv()

            @pl.when(z > 0)
            def _():
                z_send(line, False).start()

            for dx in range(1, nx):
                x_send(line, dx).start()

    load_q.wait()
    for dx in range(1, nx):
        for line in range(nz):
            kv_copy(line * nx + (x + dx) % nx, me_dp, kv_z_sem.at[0, 0]).wait_recv()

    for src in range(dp_count):
        for half, target in ((0, keys), (1, values)):
            best = kv[src, half, 0:TILE, :]
            for u in range(1, tiles):
                wanted = jnp.full((TILE, HEAD), picks[u][src]) > 0
                best = jnp.where(wanted, kv[src, half, u * TILE:(u + 1) * TILE, :].astype(F32), best.astype(F32)).astype(BF16)
            for t in range(tiles):
                target[t, (src + 1) * TILE:(src + 2) * TILE, :] = best
    for t in range(tiles):
        for half, target in ((0, keys), (1, values)):
            target[t, 0:TILE, :] = kv[me_dp, half, t * TILE:(t + 1) * TILE, :]

    pair = 2 if heads % 2 == 0 else 1
    exponent = HEAD ** (-0.5) * math.log2(math.e)
    causal = (
        lax.broadcasted_iota(jnp.int32, (TILE, TILE), 0)
        >= lax.broadcasted_iota(jnp.int32, (TILE, TILE), 1)
    )
    causal = jnp.concatenate([causal] * pair, axis=0)

    def attention(t):
        rows = slice(t * TILE, (t + 1) * TILE)

        def step(hp, carry):
            columns = pl.ds(pl.multiple_of(hp * (pair * HEAD), pair * HEAD), pair * HEAD)
            both = q[rows, columns]
            stacked = jnp.concatenate([both[:, i * HEAD:(i + 1) * HEAD] for i in range(pair)], axis=0)
            scores = lax.dot_general(stacked, keys[t], (((1,), (1,)), ((), ())), preferred_element_type=F32)
            near = jnp.where(causal, scores[:, :TILE], -jnp.inf)
            scores = jnp.concatenate([near, scores[:, TILE:] + bias[t, 0:1, TILE:]], axis=1)
            peak = jnp.max(scores, axis=1, keepdims=True)
            weights = jnp.exp2((scores - peak) * exponent)
            totals = jnp.sum(weights, axis=1, keepdims=True)
            mixed = jnp.dot(weights.astype(BF16), values[t], preferred_element_type=F32) / totals
            mixed = mixed.astype(BF16)
            att[rows, columns] = jnp.concatenate([mixed[i * TILE:(i + 1) * TILE] for i in range(pair)], axis=1)
            return carry

        lax.fori_loop(0, heads // pair, step, 0)

    def project(t, i, j):
        return jnp.dot(att[t * TILE:(t + 1) * TILE, :], w[i, :, j * WIDTH:(j + 1) * WIDTH], preferred_element_type=F32)

    def near_copy(t, dy, j):
        return pltpu.make_async_remote_copy(
            src_ref=near_send.at[dy, t, j], dst_ref=near_recv.at[dy, t, j],
            send_sem=near_send_sem.at[dy, t, j], recv_sem=near_recv_sem.at[dy, t, j],
            device_id=dev(me_dp, sibling), device_id_type=MESH)

    def far_copy(t, dy, j):
        return pltpu.make_async_remote_copy(
            src_ref=far_send.at[dy - 1, t, j], dst_ref=far_recv.at[dy - 1, t, j],
            send_sem=far_send_sem.at[dy - 1, t, j], recv_sem=far_recv_sem.at[dy - 1, t, j],
            device_id=dev(me_dp, ((y + dy) % ny) * 2 + core), device_id_type=MESH)

    def sq_copy(t, dm):
        return pltpu.make_async_remote_copy(
            src_ref=sq_send.at[t], dst_ref=sq_recv.at[t, dm - 1],
            send_sem=sq_send_sem.at[t, dm - 1], recv_sem=sq_recv_sem.at[t, dm - 1],
            device_id=dev(me_dp, (me_mp + dm) % mp_count), device_id_type=MESH)

    def give(t, dy, j):
        i = 2 * ((dy - 1) % ny)
        near_send[dy, t, j] = project(t, i, j).astype(BF16)
        near_copy(t, dy, j).start()

    def take(t, dy, j):
        i = 2 * ((dy - 1) % ny) + 1
        part = project(t, i, j)
        if dy == 0:
            own[t, j] = part
            return
        near_copy(t, dy, j).wait_recv()
        far_send[dy - 1, t, j] = (part + near_recv[dy, t, j].astype(F32)).astype(BF16)
        far_copy(t, dy, j).start()

    def run(t, dys):
        work = [(dy, j) for dy in dys for j in range(chunks)]
        for n in range(len(work) + 1):
            if n < len(work):
                give(t, *work[n])
            if n > 0:
                take(t, *work[n - 1])

    far_dys = list(range(1, ny))
    for t in range(tiles):
        attention(t)
        if t == 0:
            for copy in w_loads:
                copy.wait()
        run(t, far_dys)
    for t in range(tiles):
        run(t, [0])

    load_res.wait()
    load_gain.wait()

    def gather(t):
        rows = slice(t * TILE, (t + 1) * TILE)
        square = jnp.zeros((TILE, HEAD), F32)
        for j in range(chunks):
            near_copy(t, 0, j).wait_recv()
            for dy in far_dys:
                far_copy(t, dy, j).wait_recv()
            total = own[t, j] + near_recv[0, t, j].astype(F32)
            for dy in far_dys:
                total = total + far_recv[dy - 1, t, j].astype(F32)
            columns = slice(j * WIDTH, (j + 1) * WIDTH)
            out = (res[rows, columns].astype(F32) + total).astype(BF16)
            hid[rows, columns] = out
            out = out.astype(F32)
            out = out * out
            for k in range(WIDTH // HEAD):
                square = square + out[:, k * HEAD:(k + 1) * HEAD]
        line = jnp.broadcast_to(jnp.sum(square, axis=1, keepdims=True), (TILE, TILE))
        sq_send[t] = jnp.transpose(line)[0:8, :]
        for dm in range(1, mp_count):
            sq_copy(t, dm).start()
        pltpu.make_async_copy(hid.at[pl.ds(t * TILE, TILE)], hidden_ref.at[pl.ds(t * TILE, TILE)], out_sem.at[0, t]).start()

    def finish(t):
        rows = slice(t * TILE, (t + 1) * TILE)
        total = sq_send[t]
        for dm in range(1, mp_count):
            sq_copy(t, dm).wait_recv()
            total = total + sq_recv[t, dm - 1]
        line = lax.rsqrt(total[0:1, :] / features + 1e-05)
        scale = jnp.transpose(jnp.broadcast_to(line, (TILE, TILE)))
        for k in range(width // HEAD):
            columns = slice(k * HEAD, (k + 1) * HEAD)
            nrm[rows, columns] = (hid[rows, columns].astype(F32) * scale * gain[0:1, columns]).astype(BF16)
        pltpu.make_async_copy(nrm.at[pl.ds(t * TILE, TILE)], normed_ref.at[pl.ds(t * TILE, TILE)], out_sem.at[1, t]).start()

    for t in range(tiles):
        gather(t)
        if t > 0:
            finish(t - 1)

    for line in range(nz):
        @pl.when((z < nz - 1) & (z >= line))
        def _():
            z_send(line, True).wait_send()

        @pl.when((z > 0) & (z <= line))
        def _():
            z_send(line, False).wait_send()

        for dx in range(1, nx):
            x_send(line, dx).wait_send()
    for t in range(tiles):
        for j in range(chunks):
            for dy in range(ny):
                near_copy(t, dy, j).wait_send()
            for dy in far_dys:
                far_copy(t, dy, j).wait_send()
    finish(tiles - 1)
    for t in range(tiles):
        for dm in range(1, mp_count):
            sq_copy(t, dm).wait_send()
        pltpu.make_async_copy(hid.at[pl.ds(t * TILE, TILE)], hidden_ref.at[pl.ds(t * TILE, TILE)], out_sem.at[0, t]).wait()
        pltpu.make_async_copy(nrm.at[pl.ds(t * TILE, TILE)], normed_ref.at[pl.ds(t * TILE, TILE)], out_sem.at[1, t]).wait()


def solution(mesh):
    dp_count, mp_count = mesh.shape["dp"], mesh.shape["mp"]
    nx = 2 ** (int(math.log2(dp_count)) // 2)
    if dp_count % nx:
        nx = 1
    ny = mp_count // 2

    def body(query, keys_values, ancestors, tile_of_slot, residual, norm_gain, out_weight):
        tokens, inner = query.shape
        tiles, heads = tokens // TILE, inner // HEAD
        width = residual.shape[1]
        kv_heads = keys_values.shape[2] // HEAD
        chunks = width // WIDTH
        sizes = (dp_count, mp_count, nx, tiles, heads, kv_heads, width)
        dma = pltpu.SemaphoreType.DMA
        anywhere = pl.BlockSpec(memory_space=pl.ANY)
        smem = pl.BlockSpec(memory_space=pltpu.SMEM)
        span = (dp_count + 1) * TILE
        nz = dp_count // nx
        fy = max(ny - 1, 1)
        return pl.pallas_call(
            functools.partial(kernel, sizes),
            out_shape=(jax.ShapeDtypeStruct(residual.shape, BF16),) * 2,
            in_specs=[smem, smem] + [anywhere] * 5,
            out_specs=(anywhere, anywhere),
            scratch_shapes=[
                pltpu.VMEM((dp_count, 2, tokens, HEAD), BF16),
                pltpu.VMEM((tiles, span, HEAD), BF16),
                pltpu.VMEM((tiles, span, HEAD), BF16),
                pltpu.VMEM((tiles, 8, span), F32),
                pltpu.VMEM((tokens, inner), BF16),
                pltpu.VMEM((tokens, width), BF16),
                pltpu.VMEM((1, width), F32),
                pltpu.VMEM((mp_count, inner, width), BF16),
                pltpu.VMEM((tokens, inner), BF16),
                pltpu.VMEM((ny, tiles, chunks, TILE, WIDTH), BF16),
                pltpu.VMEM((ny, tiles, chunks, TILE, WIDTH), BF16),
                pltpu.VMEM((fy, tiles, chunks, TILE, WIDTH), BF16),
                pltpu.VMEM((fy, tiles, chunks, TILE, WIDTH), BF16),
                pltpu.VMEM((tiles, chunks, TILE, WIDTH), F32),
                pltpu.VMEM((tokens, width), BF16),
                pltpu.VMEM((tokens, width), BF16),
                pltpu.VMEM((tiles, 8, TILE), F32),
                pltpu.VMEM((tiles, mp_count - 1, 8, TILE), F32),
                dma((4,)), dma((mp_count,)), dma((2, tiles)),
                dma((dp_count,)), dma((2, nz)), dma((max(nx - 1, 1), nz)),
                dma((ny, tiles, chunks)), dma((ny, tiles, chunks)),
                dma((fy, tiles, chunks)), dma((fy, tiles, chunks)),
                dma((tiles, mp_count - 1)), dma((tiles, mp_count - 1)),
            ],
            compiler_params=pltpu.CompilerParams(
                collective_id=0, has_side_effects=True, vmem_limit_bytes=56 * 1024 * 1024),
        )(ancestors, tile_of_slot, query, keys_values, residual, norm_gain.reshape(1, width), out_weight)

    return jax.shard_map(
        body,
        mesh=mesh,
        in_specs=(
            P("dp", "mp"),
            P(None, "dp", None),
            P("dp", None),
            P(),
            P("dp", "mp"),
            P("mp"),
            P("mp", None),
        ),
        out_specs=(P("dp", "mp"), P("dp", "mp")),
        check_vma=False,
    )
```

```python
import functools
import math

import jax
import jax.numpy as jnp
from jax import lax
from jax.experimental import pallas as pl
from jax.experimental.pallas import tpu as pltpu
from jax.sharding import PartitionSpec as P

HEAD = 128
TILE = 128
WIDTH = 512
F32 = jnp.float32
BF16 = jnp.bfloat16
MESH = pl.DeviceIdType.MESH


def kernel(
    sizes,
    anc_ref, slots_ref, query_ref, pairs_ref, residual_ref, weight_ref,
    hidden_ref, total_ref,
    kv, far, stage, want, want_recv, bias, q, res, w, att, near_send, near_recv,
    far_send, far_recv, own, hid, sq_send, sq_recv,
    load_sem, w_sem, out_sem, kv_recv_sem, kv_z_sem, kv_x_sem,
    x_recv_sem, want_send_sem, want_recv_sem,
    near_send_sem, near_recv_sem, far_send_sem, far_recv_sem, sq_send_sem, sq_recv_sem,
):
    dp_count, mp_count, nx, tiles, heads, kv_heads, width = sizes
    nz = dp_count // nx
    ny = mp_count // 2
    features = mp_count * width
    chunks = width // WIDTH
    me_dp, me_mp = lax.axis_index("dp"), lax.axis_index("mp")
    z, x = me_dp // nx, me_dp % nx
    y, core = me_mp // 2, me_mp % 2
    sibling = y * 2 + (1 - core)

    def dev(dp, mp):
        return {"dp": dp, "mp": mp}

    kv_head = me_mp * kv_heads // mp_count
    own_kv = pltpu.make_async_copy(
        pairs_ref.at[:, :, pl.ds(pl.multiple_of(kv_head * HEAD, HEAD), HEAD)],
        kv.at[me_dp], load_sem.at[0])
    own_kv.start()
    load_q = pltpu.make_async_copy(query_ref, q, load_sem.at[1])
    load_q.start()
    blocks = []
    for dy in list(range(1, ny)) + [0]:
        for other in (1, 0):
            block = ((y + dy) % ny) * 2 + (core if other == 0 else 1 - core)
            blocks.append(block)
    w_loads = []
    for i, block in enumerate(blocks):
        copy = pltpu.make_async_copy(
            weight_ref.at[:, pl.ds(pl.multiple_of(block * width, width), width)],
            w.at[i], w_sem.at[i])
        copy.start()
        w_loads.append(copy)
    load_res = pltpu.make_async_copy(residual_ref, res, load_sem.at[2])
    load_res.start()

    barrier = pltpu.get_barrier_semaphore()
    for dm in range(1, mp_count):
        pl.semaphore_signal(barrier, inc=1, device_id=dev(me_dp, (me_mp + dm) % mp_count), device_id_type=MESH)
    for dx in range(1, nx):
        pl.semaphore_signal(barrier, inc=1, device_id=dev(z * nx + (x + dx) % nx, me_mp), device_id_type=MESH)

    @pl.when(z > 0)
    def _():
        pl.semaphore_signal(barrier, inc=1, device_id=dev(me_dp - nx, me_mp), device_id_type=MESH)

    @pl.when(z < nz - 1)
    def _():
        pl.semaphore_signal(barrier, inc=1, device_id=dev(me_dp + nx, me_mp), device_id_type=MESH)

    ends = jnp.where(z > 0, 1, 0) + jnp.where(z < nz - 1, 1, 0)
    pl.semaphore_wait(barrier, mp_count - 1 + nx - 1 + ends)
    own_kv.wait()

    def z_copy(src, half, target, send_sem):
        return pltpu.make_async_remote_copy(
            src_ref=kv.at[src, half], dst_ref=kv.at[src, half], send_sem=send_sem,
            recv_sem=kv_recv_sem.at[half, src], device_id=dev(target, me_mp), device_id_type=MESH)

    def z_send(line, half, up):
        return z_copy(line * nx + x, half, me_dp + (nx if up else -nx), kv_z_sem.at[1 if up else 0, half, line])

    def z_arrived(line, half):
        z_copy(line * nx + x, half, me_dp, kv_z_sem.at[0, 0, 0]).wait_recv()

    def x_copy(line, half, dx, src):
        return pltpu.make_async_remote_copy(
            src_ref=stage.at[dx - 1, line, half],
            dst_ref=far.at[half, pl.ds(pl.multiple_of(src * TILE, TILE), TILE)],
            send_sem=kv_x_sem.at[dx - 1, half, line], recv_sem=x_recv_sem.at[half, src],
            device_id=dev(z * nx + (x + dx) % nx, me_mp), device_id_type=MESH)

    def want_copy(dx):
        return pltpu.make_async_remote_copy(
            src_ref=want, dst_ref=want_recv.at[dx - 1],
            send_sem=want_send_sem.at[dx - 1], recv_sem=want_recv_sem.at[dx - 1],
            device_id=dev(z * nx + (x + dx) % nx, me_mp), device_id_type=MESH)

    def select(src, half, pick):
        pick = jnp.broadcast_to(pick, (TILE, HEAD))
        best = kv[src, half, 0:TILE, :].astype(F32)
        for u in range(1, tiles):
            best = jnp.where(pick == u, kv[src, half, u * TILE:(u + 1) * TILE, :].astype(F32), best)
        return best.astype(BF16)

    def deliver(line, half):
        src = line * nx + x
        for dx in range(1, nx):
            stage[dx - 1, line, half] = select(src, half, want_recv[nx - dx - 1, src, 0:1, :])
            x_copy(line, half, dx, src).start()
        far[half, pl.ds(pl.multiple_of(src * TILE, TILE), TILE), :] = select(src, half, want[src, 0:1, :])

    for half in range(2):
        @pl.when(z < nz - 1)
        def _():
            z_send(z, half, True).start()

        @pl.when(z > 0)
        def _():
            z_send(z, half, False).start()

    def lookup(src, carry):
        picked = jnp.int32(0)
        seen = [jnp.int32(0)] * tiles
        for u in range(tiles):
            slot = src * tiles + u
            tile_id = slots_ref[slot]
            hit = jnp.int32(0)
            for t in range(tiles):
                found = jnp.int32(0)
                for j in range(anc_ref.shape[1]):
                    found = found | jnp.where(anc_ref[t, j] == tile_id, 1, 0)
                found = found * jnp.where(slot == me_dp * tiles + t, 0, 1)
                seen[t] = seen[t] | found
                hit = hit | found
            picked = picked + hit * u
        for t in range(tiles):
            column = jnp.where(jnp.full((8, TILE), seen[t]) > 0, 0.0, -jnp.inf).astype(F32)
            bias[t, :, pl.ds(pl.multiple_of(src * TILE, TILE), TILE)] = column
        want[src] = jnp.full((8, TILE), picked).astype(F32)
        return carry

    lax.fori_loop(0, dp_count, lookup, 0)
    for dx in range(1, nx):
        want_copy(dx).start()

    for d in range(1, nz):
        for half in range(2):
            @pl.when(z >= d)
            def _():
                z_arrived(z - d, half)

                @pl.when(z < nz - 1)
                def _():
                    z_send(z - d, half, True).start()

            @pl.when(z + d < nz)
            def _():
                z_arrived(z + d, half)

                @pl.when(z > 0)
                def _():
                    z_send(z + d, half, False).start()

            if d == 1 and half == 0:
                for dx in range(1, nx):
                    want_copy(dx).wait_recv()
                for part in range(2):
                    deliver(z, part)

            @pl.when(z >= d)
            def _():
                deliver(z - d, half)

            @pl.when(z + d < nz)
            def _():
                deliver(z + d, half)

    if nz == 1:
        for dx in range(1, nx):
            want_copy(dx).wait_recv()
        for part in range(2):
            deliver(z, part)

    load_q.wait()
    for dx in range(1, nx):
        for line in range(nz):
            for half in range(2):
                x_copy(line, half, dx, line * nx + (x + dx) % nx).wait_recv()

    pair = 2 if heads % 2 == 0 else 1
    exponent = HEAD ** (-0.5) * math.log2(math.e)
    causal = (
        lax.broadcasted_iota(jnp.int32, (TILE, TILE), 0)
        >= lax.broadcasted_iota(jnp.int32, (TILE, TILE), 1)
    )
    causal = jnp.concatenate([causal] * pair, axis=0)

    def attention(t):
        rows = slice(t * TILE, (t + 1) * TILE)

        def step(hp, carry):
            columns = pl.ds(pl.multiple_of(hp * (pair * HEAD), pair * HEAD), pair * HEAD)
            both = q[rows, columns]
            stacked = jnp.concatenate([both[:, i * HEAD:(i + 1) * HEAD] for i in range(pair)], axis=0)
            near = lax.dot_general(
                stacked, kv[me_dp, 0, rows, :], (((1,), (1,)), ((), ())), preferred_element_type=F32)
            scores = lax.dot_general(stacked, far[0], (((1,), (1,)), ((), ())), preferred_element_type=F32)
            near = jnp.where(causal, near, -jnp.inf)
            scores = scores + bias[t, 0:1, :]
            peak = jnp.maximum(jnp.max(scores, axis=1, keepdims=True), jnp.max(near, axis=1, keepdims=True))
            near = jnp.exp2((near - peak) * exponent)
            weights = jnp.exp2((scores - peak) * exponent)
            totals = jnp.sum(weights, axis=1, keepdims=True) + jnp.sum(near, axis=1, keepdims=True)
            mixed = jnp.dot(weights.astype(BF16), far[1], preferred_element_type=F32)
            mixed = mixed + jnp.dot(near.astype(BF16), kv[me_dp, 1, rows, :], preferred_element_type=F32)
            mixed = mixed / totals
            mixed = mixed.astype(BF16)
            att[rows, columns] = jnp.concatenate([mixed[i * TILE:(i + 1) * TILE] for i in range(pair)], axis=1)
            return carry

        lax.fori_loop(0, heads // pair, step, 0)

    def project(t, i, j):
        return jnp.dot(att[t * TILE:(t + 1) * TILE, :], w[i, :, j * WIDTH:(j + 1) * WIDTH], preferred_element_type=F32)

    def near_copy(t, dy, j):
        return pltpu.make_async_remote_copy(
            src_ref=near_send.at[dy, t, j], dst_ref=near_recv.at[dy, t, j],
            send_sem=near_send_sem.at[dy, t, j], recv_sem=near_recv_sem.at[dy, t, j],
            device_id=dev(me_dp, sibling), device_id_type=MESH)

    def far_copy(t, dy, j):
        return pltpu.make_async_remote_copy(
            src_ref=far_send.at[dy - 1, t, j], dst_ref=far_recv.at[dy - 1, t, j],
            send_sem=far_send_sem.at[dy - 1, t, j], recv_sem=far_recv_sem.at[dy - 1, t, j],
            device_id=dev(me_dp, ((y + dy) % ny) * 2 + core), device_id_type=MESH)

    def sq_copy(t, dm):
        return pltpu.make_async_remote_copy(
            src_ref=sq_send.at[t], dst_ref=sq_recv.at[t, dm - 1],
            send_sem=sq_send_sem.at[t, dm - 1], recv_sem=sq_recv_sem.at[t, dm - 1],
            device_id=dev(me_dp, (me_mp + dm) % mp_count), device_id_type=MESH)

    def give(t, dy, j):
        i = 2 * ((dy - 1) % ny)
        near_send[dy, t, j] = project(t, i, j).astype(BF16)
        near_copy(t, dy, j).start()

    def take(t, dy, j):
        i = 2 * ((dy - 1) % ny) + 1
        part = project(t, i, j)
        if dy == 0:
            own[t, j] = part
            return
        near_copy(t, dy, j).wait_recv()
        far_send[dy - 1, t, j] = (part + near_recv[dy, t, j].astype(F32)).astype(BF16)
        far_copy(t, dy, j).start()

    def run(t, dys):
        work = [(dy, j) for dy in dys for j in range(chunks)]
        for n in range(len(work) + 1):
            if n < len(work):
                give(t, *work[n])
            if n > 0:
                take(t, *work[n - 1])

    far_dys = list(range(1, ny))
    for t in range(tiles):
        attention(t)
        if t == 0:
            for copy in w_loads:
                copy.wait()
        run(t, far_dys)
    for t in range(tiles):
        run(t, [0])

    load_res.wait()

    def gather(t):
        rows = slice(t * TILE, (t + 1) * TILE)
        square = jnp.zeros((TILE, HEAD), F32)
        for j in range(chunks):
            near_copy(t, 0, j).wait_recv()
            for dy in far_dys:
                far_copy(t, dy, j).wait_recv()
            total = own[t, j] + near_recv[0, t, j].astype(F32)
            for dy in far_dys:
                total = total + far_recv[dy - 1, t, j].astype(F32)
            columns = slice(j * WIDTH, (j + 1) * WIDTH)
            out = (res[rows, columns].astype(F32) + total).astype(BF16)
            hid[rows, columns] = out
            out = out.astype(F32)
            out = out * out
            for k in range(WIDTH // HEAD):
                square = square + out[:, k * HEAD:(k + 1) * HEAD]
        line = jnp.broadcast_to(jnp.sum(square, axis=1, keepdims=True), (TILE, TILE))
        sq_send[t] = jnp.transpose(line)[0:8, :]
        for dm in range(1, mp_count):
            sq_copy(t, dm).start()
        pltpu.make_async_copy(hid.at[pl.ds(t * TILE, TILE)], hidden_ref.at[pl.ds(t * TILE, TILE)], out_sem.at[t]).start()

    def finish(t):
        total = sq_send[t]
        for dm in range(1, mp_count):
            sq_copy(t, dm).wait_recv()
            total = total + sq_recv[t, dm - 1]
        total_ref[t] = total

    for t in range(tiles):
        gather(t)
        if t > 0:
            finish(t - 1)

    for line in range(nz):
        for half in range(2):
            @pl.when((z < nz - 1) & (z >= line))
            def _():
                z_send(line, half, True).wait_send()

            @pl.when((z > 0) & (z <= line))
            def _():
                z_send(line, half, False).wait_send()

            for dx in range(1, nx):
                x_copy(line, half, dx, me_dp).wait_send()
    for dx in range(1, nx):
        want_copy(dx).wait_send()
    for t in range(tiles):
        for j in range(chunks):
            for dy in range(ny):
                near_copy(t, dy, j).wait_send()
            for dy in far_dys:
                far_copy(t, dy, j).wait_send()
    finish(tiles - 1)
    for t in range(tiles):
        for dm in range(1, mp_count):
            sq_copy(t, dm).wait_send()
        pltpu.make_async_copy(hid.at[pl.ds(t * TILE, TILE)], hidden_ref.at[pl.ds(t * TILE, TILE)], out_sem.at[t]).wait()


def norm_kernel(features, hidden_ref, total_ref, gain_ref, out_ref, normed_ref, hid, nrm, in_sem, out_sem):
    tiles = total_ref.shape[0]

    def part(t):
        return pl.ds(t * TILE, TILE)

    for t in range(tiles):
        pltpu.make_async_copy(hidden_ref.at[part(t)], hid.at[part(t)], in_sem.at[t]).start()
    for t in range(tiles):
        rows = slice(t * TILE, (t + 1) * TILE)
        line = lax.rsqrt(total_ref[t, 0:1, :] / features + 1e-05)
        scale = jnp.transpose(jnp.broadcast_to(line, (TILE, TILE)))
        pltpu.make_async_copy(hidden_ref.at[part(t)], hid.at[part(t)], in_sem.at[t]).wait()
        pltpu.make_async_copy(hid.at[part(t)], out_ref.at[part(t)], out_sem.at[0, t]).start()
        for k in range(gain_ref.shape[1] // HEAD):
            columns = slice(k * HEAD, (k + 1) * HEAD)
            nrm[rows, columns] = (hid[rows, columns].astype(F32) * scale * gain_ref[0:1, columns]).astype(BF16)
        pltpu.make_async_copy(nrm.at[part(t)], normed_ref.at[part(t)], out_sem.at[1, t]).start()
    for t in range(tiles):
        pltpu.make_async_copy(hid.at[part(t)], out_ref.at[part(t)], out_sem.at[0, t]).wait()
        pltpu.make_async_copy(nrm.at[part(t)], normed_ref.at[part(t)], out_sem.at[1, t]).wait()


def solution(mesh):
    dp_count, mp_count = mesh.shape["dp"], mesh.shape["mp"]
    nx = 2 ** (int(math.log2(dp_count)) // 2)
    if dp_count % nx:
        nx = 1
    ny = mp_count // 2

    def body(query, keys_values, ancestors, tile_of_slot, residual, norm_gain, out_weight):
        tokens, inner = query.shape
        tiles, heads = tokens // TILE, inner // HEAD
        width = residual.shape[1]
        kv_heads = keys_values.shape[2] // HEAD
        chunks = width // WIDTH
        sizes = (dp_count, mp_count, nx, tiles, heads, kv_heads, width)
        dma = pltpu.SemaphoreType.DMA
        anywhere = pl.BlockSpec(memory_space=pl.ANY)
        smem = pl.BlockSpec(memory_space=pltpu.SMEM)
        span = dp_count * TILE
        fx = max(nx - 1, 1)
        vmem = pl.BlockSpec(memory_space=pltpu.VMEM)
        nz = dp_count // nx
        fy = max(ny - 1, 1)
        hidden, total = pl.pallas_call(
            functools.partial(kernel, sizes),
            out_shape=(jax.ShapeDtypeStruct(residual.shape, BF16), jax.ShapeDtypeStruct((tiles, 8, TILE), F32)),
            in_specs=[smem, smem] + [anywhere] * 4,
            out_specs=(anywhere, vmem),
            scratch_shapes=[
                pltpu.VMEM((dp_count, 2, tokens, HEAD), BF16),
                pltpu.VMEM((2, span, HEAD), BF16),
                pltpu.VMEM((fx, nz, 2, TILE, HEAD), BF16),
                pltpu.VMEM((dp_count, 8, TILE), F32),
                pltpu.VMEM((fx, dp_count, 8, TILE), F32),
                pltpu.VMEM((tiles, 8, span), F32),
                pltpu.VMEM((tokens, inner), BF16),
                pltpu.VMEM((tokens, width), BF16),
                pltpu.VMEM((mp_count, inner, width), BF16),
                pltpu.VMEM((tokens, inner), BF16),
                pltpu.VMEM((ny, tiles, chunks, TILE, WIDTH), BF16),
                pltpu.VMEM((ny, tiles, chunks, TILE, WIDTH), BF16),
                pltpu.VMEM((fy, tiles, chunks, TILE, WIDTH), BF16),
                pltpu.VMEM((fy, tiles, chunks, TILE, WIDTH), BF16),
                pltpu.VMEM((tiles, chunks, TILE, WIDTH), F32),
                pltpu.VMEM((tokens, width), BF16),
                pltpu.VMEM((tiles, 8, TILE), F32),
                pltpu.VMEM((tiles, mp_count - 1, 8, TILE), F32),
                dma((4,)), dma((mp_count,)), dma((tiles,)),
                dma((2, dp_count)), dma((2, 2, nz)), dma((fx, 2, nz)),
                dma((2, dp_count)), dma((fx,)), dma((fx,)),
                dma((ny, tiles, chunks)), dma((ny, tiles, chunks)),
                dma((fy, tiles, chunks)), dma((fy, tiles, chunks)),
                dma((tiles, mp_count - 1)), dma((tiles, mp_count - 1)),
            ],
            compiler_params=pltpu.CompilerParams(
                collective_id=0, has_side_effects=True, vmem_limit_bytes=56 * 1024 * 1024),
        )(ancestors, tile_of_slot, query, keys_values, residual, out_weight)
        return pl.pallas_call(
            functools.partial(norm_kernel, mp_count * width),
            out_shape=(jax.ShapeDtypeStruct(residual.shape, BF16),) * 2,
            in_specs=[anywhere, vmem, vmem],
            out_specs=(anywhere, anywhere),
            scratch_shapes=[
                pltpu.VMEM((tokens, width), BF16),
                pltpu.VMEM((tokens, width), BF16),
                dma((tiles,)), dma((2, tiles)),
            ],
            compiler_params=pltpu.CompilerParams(vmem_limit_bytes=56 * 1024 * 1024),
        )(hidden, total, norm_gain.reshape(1, width))

    return jax.shard_map(
        body,
        mesh=mesh,
        in_specs=(
            P("dp", "mp"),
            P(None, "dp", None),
            P("dp", None),
            P(),
            P("dp", "mp"),
            P("mp"),
            P("mp", None),
        ),
        out_specs=(P("dp", "mp"), P("dp", "mp")),
        check_vma=False,
    )
```

```python
import functools
import math

import jax
import jax.numpy as jnp
from jax import lax
from jax.experimental import pallas as pl
from jax.experimental.pallas import tpu as pltpu
from jax.sharding import PartitionSpec as P

HEAD = 128
TILE = 128
WIDTH = 512
F32 = jnp.float32
BF16 = jnp.bfloat16
MESH = pl.DeviceIdType.MESH


def kernel(
    sizes,
    anc_ref, slots_ref, query_ref, pairs_ref, residual_ref, weight_ref,
    hidden_ref, total_ref,
    kv, far, stage, want, want_recv, bias, q, res, w, att, near_send, near_recv,
    far_send, far_recv, own, hid, sq_send, sq_recv,
    load_sem, w_sem, out_sem, kv_recv_sem, kv_z_sem, kv_x_sem,
    x_recv_sem, want_send_sem, want_recv_sem,
    near_send_sem, near_recv_sem, far_send_sem, far_recv_sem, sq_send_sem, sq_recv_sem,
):
    dp_count, mp_count, nx, tiles, heads, kv_heads, width = sizes
    nz = dp_count // nx
    ny = mp_count // 2
    features = mp_count * width
    chunks = width // WIDTH
    me_dp, me_mp = lax.axis_index("dp"), lax.axis_index("mp")
    z, x = me_dp // nx, me_dp % nx
    y, core = me_mp // 2, me_mp % 2
    sibling = y * 2 + (1 - core)

    def dev(dp, mp):
        return {"dp": dp, "mp": mp}

    kv_head = me_mp * kv_heads // mp_count
    own_kv = pltpu.make_async_copy(
        pairs_ref.at[:, :, pl.ds(pl.multiple_of(kv_head * HEAD, HEAD), HEAD)],
        kv.at[me_dp], load_sem.at[0])
    own_kv.start()
    load_q = pltpu.make_async_copy(query_ref, q, load_sem.at[1])
    load_q.start()
    blocks = []
    for dy in list(range(1, ny)) + [0]:
        for other in (1, 0):
            block = ((y + dy) % ny) * 2 + (core if other == 0 else 1 - core)
            blocks.append(block)
    w_loads = []
    for i, block in enumerate(blocks):
        copy = pltpu.make_async_copy(
            weight_ref.at[:, pl.ds(pl.multiple_of(block * width, width), width)],
            w.at[i], w_sem.at[i])
        copy.start()
        w_loads.append(copy)
    load_res = pltpu.make_async_copy(residual_ref, res, load_sem.at[2])
    load_res.start()

    barrier = pltpu.get_barrier_semaphore()
    for dm in range(1, mp_count):
        pl.semaphore_signal(barrier, inc=1, device_id=dev(me_dp, (me_mp + dm) % mp_count), device_id_type=MESH)
    for dx in range(1, nx):
        pl.semaphore_signal(barrier, inc=1, device_id=dev(z * nx + (x + dx) % nx, me_mp), device_id_type=MESH)

    @pl.when(z > 0)
    def _():
        pl.semaphore_signal(barrier, inc=1, device_id=dev(me_dp - nx, me_mp), device_id_type=MESH)

    @pl.when(z < nz - 1)
    def _():
        pl.semaphore_signal(barrier, inc=1, device_id=dev(me_dp + nx, me_mp), device_id_type=MESH)

    ends = jnp.where(z > 0, 1, 0) + jnp.where(z < nz - 1, 1, 0)
    pl.semaphore_wait(barrier, mp_count - 1 + nx - 1 + ends)
    own_kv.wait()

    def z_copy(src, half, target, send_sem):
        return pltpu.make_async_remote_copy(
            src_ref=kv.at[src, half], dst_ref=kv.at[src, half], send_sem=send_sem,
            recv_sem=kv_recv_sem.at[half, src], device_id=dev(target, me_mp), device_id_type=MESH)

    def z_send(line, half, up):
        return z_copy(line * nx + x, half, me_dp + (nx if up else -nx), kv_z_sem.at[1 if up else 0, half, line])

    def z_arrived(line, half):
        z_copy(line * nx + x, half, me_dp, kv_z_sem.at[0, 0, 0]).wait_recv()

    def x_copy(line, half, dx, src):
        return pltpu.make_async_remote_copy(
            src_ref=stage.at[dx - 1, line, half],
            dst_ref=far.at[half, pl.ds(pl.multiple_of(src * TILE, TILE), TILE)],
            send_sem=kv_x_sem.at[dx - 1, half, line], recv_sem=x_recv_sem.at[half, src],
            device_id=dev(z * nx + (x + dx) % nx, me_mp), device_id_type=MESH)

    def want_copy(dx):
        return pltpu.make_async_remote_copy(
            src_ref=want, dst_ref=want_recv.at[dx - 1],
            send_sem=want_send_sem.at[dx - 1], recv_sem=want_recv_sem.at[dx - 1],
            device_id=dev(z * nx + (x + dx) % nx, me_mp), device_id_type=MESH)

    def select(src, half, pick):
        pick = jnp.broadcast_to(pick, (TILE, HEAD))
        best = kv[src, half, 0:TILE, :].astype(F32)
        for u in range(1, tiles):
            best = jnp.where(pick == u, kv[src, half, u * TILE:(u + 1) * TILE, :].astype(F32), best)
        return best.astype(BF16)

    def deliver(line, half):
        src = line * nx + x
        for dx in range(1, nx):
            stage[dx - 1, line, half] = select(src, half, want_recv[nx - dx - 1, src, 0:1, :])
            x_copy(line, half, dx, src).start()
        far[half, pl.ds(pl.multiple_of(src * TILE, TILE), TILE), :] = select(src, half, want[src, 0:1, :])

    for half in range(2):
        @pl.when(z < nz - 1)
        def _():
            z_send(z, half, True).start()

        @pl.when(z > 0)
        def _():
            z_send(z, half, False).start()

    def lookup(src, carry):
        picked = jnp.int32(0)
        seen = [jnp.int32(0)] * tiles
        for u in range(tiles):
            slot = src * tiles + u
            tile_id = slots_ref[slot]
            hit = jnp.int32(0)
            for t in range(tiles):
                found = jnp.int32(0)
                for j in range(anc_ref.shape[1]):
                    found = found | jnp.where(anc_ref[t, j] == tile_id, 1, 0)
                found = found * jnp.where(slot == me_dp * tiles + t, 0, 1)
                seen[t] = seen[t] | found
                hit = hit | found
            picked = picked + hit * u
        for t in range(tiles):
            column = jnp.where(jnp.full((8, TILE), seen[t]) > 0, 0.0, -jnp.inf).astype(F32)
            bias[t, :, pl.ds(pl.multiple_of(src * TILE, TILE), TILE)] = column
        want[src] = jnp.full((8, TILE), picked).astype(F32)
        return carry

    lax.fori_loop(0, dp_count, lookup, 0)
    for dx in range(1, nx):
        want_copy(dx).start()

    for d in range(1, nz):
        for half in range(2):
            @pl.when(z >= d)
            def _():
                z_arrived(z - d, half)

                @pl.when(z < nz - 1)
                def _():
                    z_send(z - d, half, True).start()

            @pl.when(z + d < nz)
            def _():
                z_arrived(z + d, half)

                @pl.when(z > 0)
                def _():
                    z_send(z + d, half, False).start()

            if half == 1 and d == 1:
                for dx in range(1, nx):
                    want_copy(dx).wait_recv()
                for part in range(2):
                    deliver(z, part)

            ready = [half] if d == nz - 1 else [0, 1] if half == 1 else []
            if d == 1 and half == 0:
                ready = []
            elif d == 1 and half == 1:
                ready = [0, 1]
            for part in ready:
                @pl.when(z >= d)
                def _():
                    deliver(z - d, part)

                @pl.when(z + d < nz)
                def _():
                    deliver(z + d, part)

    if nz == 1:
        for dx in range(1, nx):
            want_copy(dx).wait_recv()
        for part in range(2):
            deliver(z, part)

    load_q.wait()
    for dx in range(1, nx):
        for line in range(nz):
            for half in range(2):
                x_copy(line, half, dx, line * nx + (x + dx) % nx).wait_recv()

    pair = 2 if heads % 2 == 0 else 1
    exponent = HEAD ** (-0.5) * math.log2(math.e)
    causal = (
        lax.broadcasted_iota(jnp.int32, (TILE, TILE), 0)
        >= lax.broadcasted_iota(jnp.int32, (TILE, TILE), 1)
    )
    causal = jnp.concatenate([causal] * pair, axis=0)

    def attention(t):
        rows = slice(t * TILE, (t + 1) * TILE)

        def step(hp, carry):
            columns = pl.ds(pl.multiple_of(hp * (pair * HEAD), pair * HEAD), pair * HEAD)
            both = q[rows, columns]
            stacked = jnp.concatenate([both[:, i * HEAD:(i + 1) * HEAD] for i in range(pair)], axis=0)
            near = lax.dot_general(
                stacked, kv[me_dp, 0, rows, :], (((1,), (1,)), ((), ())), preferred_element_type=F32)
            scores = lax.dot_general(stacked, far[0], (((1,), (1,)), ((), ())), preferred_element_type=F32)
            near = jnp.where(causal, near, -jnp.inf)
            scores = scores + bias[t, 0:1, :]
            peak = jnp.maximum(jnp.max(scores, axis=1, keepdims=True), jnp.max(near, axis=1, keepdims=True))
            near = jnp.exp2((near - peak) * exponent)
            weights = jnp.exp2((scores - peak) * exponent)
            totals = jnp.sum(weights, axis=1, keepdims=True) + jnp.sum(near, axis=1, keepdims=True)
            mixed = jnp.dot(weights.astype(BF16), far[1], preferred_element_type=F32)
            mixed = mixed + jnp.dot(near.astype(BF16), kv[me_dp, 1, rows, :], preferred_element_type=F32)
            mixed = mixed / totals
            mixed = mixed.astype(BF16)
            att[rows, columns] = jnp.concatenate([mixed[i * TILE:(i + 1) * TILE] for i in range(pair)], axis=1)
            return carry

        lax.fori_loop(0, heads // pair, step, 0, unroll=True)

    def project(t, i, j):
        return jnp.dot(att[t * TILE:(t + 1) * TILE, :], w[i, :, j * WIDTH:(j + 1) * WIDTH], preferred_element_type=F32)

    def near_copy(t, dy, j):
        return pltpu.make_async_remote_copy(
            src_ref=near_send.at[dy, t, j], dst_ref=near_recv.at[dy, t, j],
            send_sem=near_send_sem.at[dy, t, j], recv_sem=near_recv_sem.at[dy, t, j],
            device_id=dev(me_dp, sibling), device_id_type=MESH)

    def far_copy(t, dy, j):
        return pltpu.make_async_remote_copy(
            src_ref=far_send.at[dy - 1, t, j], dst_ref=far_recv.at[dy - 1, t, j],
            send_sem=far_send_sem.at[dy - 1, t, j], recv_sem=far_recv_sem.at[dy - 1, t, j],
            device_id=dev(me_dp, ((y + dy) % ny) * 2 + core), device_id_type=MESH)

    def sq_copy(t, dm):
        return pltpu.make_async_remote_copy(
            src_ref=sq_send.at[t], dst_ref=sq_recv.at[t, dm - 1],
            send_sem=sq_send_sem.at[t, dm - 1], recv_sem=sq_recv_sem.at[t, dm - 1],
            device_id=dev(me_dp, (me_mp + dm) % mp_count), device_id_type=MESH)

    def give(t, dy, j):
        i = 2 * ((dy - 1) % ny)
        near_send[dy, t, j] = project(t, i, j).astype(BF16)
        near_copy(t, dy, j).start()

    def take(t, dy, j):
        i = 2 * ((dy - 1) % ny) + 1
        part = project(t, i, j)
        if dy == 0:
            own[t, j] = part
            return
        near_copy(t, dy, j).wait_recv()
        far_send[dy - 1, t, j] = (part + near_recv[dy, t, j].astype(F32)).astype(BF16)
        far_copy(t, dy, j).start()

    def run(t, dys):
        work = [(dy, j) for dy in dys for j in range(chunks)]
        for n in range(len(work) + 1):
            if n < len(work):
                give(t, *work[n])
            if n > 0:
                take(t, *work[n - 1])

    far_dys = list(range(1, ny))
    for t in range(tiles):
        attention(t)
        if t == 0:
            for copy in w_loads:
                copy.wait()
        run(t, far_dys)
    for t in range(tiles):
        run(t, [0])

    load_res.wait()

    def gather(t):
        rows = slice(t * TILE, (t + 1) * TILE)
        square = jnp.zeros((TILE, HEAD), F32)
        for j in range(chunks):
            near_copy(t, 0, j).wait_recv()
            for dy in far_dys:
                far_copy(t, dy, j).wait_recv()
            total = own[t, j] + near_recv[0, t, j].astype(F32)
            for dy in far_dys:
                total = total + far_recv[dy - 1, t, j].astype(F32)
            columns = slice(j * WIDTH, (j + 1) * WIDTH)
            out = (res[rows, columns].astype(F32) + total).astype(BF16)
            hid[rows, columns] = out
            out = out.astype(F32)
            out = out * out
            for k in range(WIDTH // HEAD):
                square = square + out[:, k * HEAD:(k + 1) * HEAD]
        line = jnp.broadcast_to(jnp.sum(square, axis=1, keepdims=True), (TILE, TILE))
        sq_send[t] = jnp.transpose(line)[0:8, :]
        for dm in range(1, mp_count):
            sq_copy(t, dm).start()
        pltpu.make_async_copy(hid.at[pl.ds(t * TILE, TILE)], hidden_ref.at[pl.ds(t * TILE, TILE)], out_sem.at[t]).start()

    def finish(t):
        total = sq_send[t]
        for dm in range(1, mp_count):
            sq_copy(t, dm).wait_recv()
            total = total + sq_recv[t, dm - 1]
        total_ref[t] = total

    for t in range(tiles):
        gather(t)
        if t > 0:
            finish(t - 1)

    for line in range(nz):
        for half in range(2):
            @pl.when((z < nz - 1) & (z >= line))
            def _():
                z_send(line, half, True).wait_send()

            @pl.when((z > 0) & (z <= line))
            def _():
                z_send(line, half, False).wait_send()

            for dx in range(1, nx):
                x_copy(line, half, dx, me_dp).wait_send()
    for dx in range(1, nx):
        want_copy(dx).wait_send()
    for t in range(tiles):
        for j in range(chunks):
            for dy in range(ny):
                near_copy(t, dy, j).wait_send()
            for dy in far_dys:
                far_copy(t, dy, j).wait_send()
    finish(tiles - 1)
    for t in range(tiles):
        for dm in range(1, mp_count):
            sq_copy(t, dm).wait_send()
        pltpu.make_async_copy(hid.at[pl.ds(t * TILE, TILE)], hidden_ref.at[pl.ds(t * TILE, TILE)], out_sem.at[t]).wait()


def norm_kernel(features, hidden_ref, total_ref, gain_ref, out_ref, normed_ref, hid, nrm, in_sem, out_sem):
    tiles = total_ref.shape[0]

    def part(t):
        return pl.ds(t * TILE, TILE)

    for t in range(tiles):
        pltpu.make_async_copy(hidden_ref.at[part(t)], hid.at[part(t)], in_sem.at[t]).start()
    for t in range(tiles):
        rows = slice(t * TILE, (t + 1) * TILE)
        line = lax.rsqrt(total_ref[t, 0:1, :] / features + 1e-05)
        scale = jnp.transpose(jnp.broadcast_to(line, (TILE, TILE)))
        pltpu.make_async_copy(hidden_ref.at[part(t)], hid.at[part(t)], in_sem.at[t]).wait()
        pltpu.make_async_copy(hid.at[part(t)], out_ref.at[part(t)], out_sem.at[0, t]).start()
        for k in range(gain_ref.shape[1] // HEAD):
            columns = slice(k * HEAD, (k + 1) * HEAD)
            nrm[rows, columns] = (hid[rows, columns].astype(F32) * scale * gain_ref[0:1, columns]).astype(BF16)
        pltpu.make_async_copy(nrm.at[part(t)], normed_ref.at[part(t)], out_sem.at[1, t]).start()
    for t in range(tiles):
        pltpu.make_async_copy(hid.at[part(t)], out_ref.at[part(t)], out_sem.at[0, t]).wait()
        pltpu.make_async_copy(nrm.at[part(t)], normed_ref.at[part(t)], out_sem.at[1, t]).wait()


def solution(mesh):
    dp_count, mp_count = mesh.shape["dp"], mesh.shape["mp"]
    nx = 2 ** (int(math.log2(dp_count)) // 2)
    if dp_count % nx:
        nx = 1
    ny = mp_count // 2

    def body(query, keys_values, ancestors, tile_of_slot, residual, norm_gain, out_weight):
        tokens, inner = query.shape
        tiles, heads = tokens // TILE, inner // HEAD
        width = residual.shape[1]
        kv_heads = keys_values.shape[2] // HEAD
        chunks = width // WIDTH
        sizes = (dp_count, mp_count, nx, tiles, heads, kv_heads, width)
        dma = pltpu.SemaphoreType.DMA
        anywhere = pl.BlockSpec(memory_space=pl.ANY)
        smem = pl.BlockSpec(memory_space=pltpu.SMEM)
        span = dp_count * TILE
        fx = max(nx - 1, 1)
        vmem = pl.BlockSpec(memory_space=pltpu.VMEM)
        nz = dp_count // nx
        fy = max(ny - 1, 1)
        hidden, total = pl.pallas_call(
            functools.partial(kernel, sizes),
            out_shape=(jax.ShapeDtypeStruct(residual.shape, BF16), jax.ShapeDtypeStruct((tiles, 8, TILE), F32)),
            in_specs=[smem, smem] + [anywhere] * 4,
            out_specs=(anywhere, vmem),
            scratch_shapes=[
                pltpu.VMEM((dp_count, 2, tokens, HEAD), BF16),
                pltpu.VMEM((2, span, HEAD), BF16),
                pltpu.VMEM((fx, nz, 2, TILE, HEAD), BF16),
                pltpu.VMEM((dp_count, 8, TILE), F32),
                pltpu.VMEM((fx, dp_count, 8, TILE), F32),
                pltpu.VMEM((tiles, 8, span), F32),
                pltpu.VMEM((tokens, inner), BF16),
                pltpu.VMEM((tokens, width), BF16),
                pltpu.VMEM((mp_count, inner, width), BF16),
                pltpu.VMEM((tokens, inner), BF16),
                pltpu.VMEM((ny, tiles, chunks, TILE, WIDTH), BF16),
                pltpu.VMEM((ny, tiles, chunks, TILE, WIDTH), BF16),
                pltpu.VMEM((fy, tiles, chunks, TILE, WIDTH), BF16),
                pltpu.VMEM((fy, tiles, chunks, TILE, WIDTH), BF16),
                pltpu.VMEM((tiles, chunks, TILE, WIDTH), F32),
                pltpu.VMEM((tokens, width), BF16),
                pltpu.VMEM((tiles, 8, TILE), F32),
                pltpu.VMEM((tiles, mp_count - 1, 8, TILE), F32),
                dma((4,)), dma((mp_count,)), dma((tiles,)),
                dma((2, dp_count)), dma((2, 2, nz)), dma((fx, 2, nz)),
                dma((2, dp_count)), dma((fx,)), dma((fx,)),
                dma((ny, tiles, chunks)), dma((ny, tiles, chunks)),
                dma((fy, tiles, chunks)), dma((fy, tiles, chunks)),
                dma((tiles, mp_count - 1)), dma((tiles, mp_count - 1)),
            ],
            compiler_params=pltpu.CompilerParams(
                collective_id=0, has_side_effects=True, vmem_limit_bytes=56 * 1024 * 1024),
        )(ancestors, tile_of_slot, query, keys_values, residual, out_weight)
        return pl.pallas_call(
            functools.partial(norm_kernel, mp_count * width),
            out_shape=(jax.ShapeDtypeStruct(residual.shape, BF16),) * 2,
            in_specs=[anywhere, vmem, vmem],
            out_specs=(anywhere, anywhere),
            scratch_shapes=[
                pltpu.VMEM((tokens, width), BF16),
                pltpu.VMEM((tokens, width), BF16),
                dma((tiles,)), dma((2, tiles)),
            ],
            compiler_params=pltpu.CompilerParams(vmem_limit_bytes=56 * 1024 * 1024),
        )(hidden, total, norm_gain.reshape(1, width))

    return jax.shard_map(
        body,
        mesh=mesh,
        in_specs=(
            P("dp", "mp"),
            P(None, "dp", None),
            P("dp", None),
            P(),
            P("dp", "mp"),
            P("mp"),
            P("mp", None),
        ),
        out_specs=(P("dp", "mp"), P("dp", "mp")),
        check_vma=False,
    )
```
